32 devices in a mesh: dom: 8 (over z, x), tensor: 4 (over y, core).
Axes of the slice: x: 2, y: 2, z: 4, core: 2. Of those that a mesh axis runs over, the one named last changes fastest.
Arguments:
- node_state: bfloat16 [2048, 512], P('dom', 'tensor'), may hold values from -6 to 6
- cotangent: bfloat16 [2048, 512], P('dom', 'tensor'), may hold values from -6 to 6
- w_in: bfloat16 [512, 1024], P('tensor'), may hold values from -0.1875 to 0.1875
- w_out: bfloat16 [512, 512], P('tensor'), may hold values from -0.25 to 0.25
- send_list: int32 [8, 7, 16], P('dom'), may hold values from 0 to 255
- sender: int32 [12288], P('dom'), may hold values from 0 to 367
- receiver: int32 [12288], P('dom'), may hold values from 0 to 255
- edge_count: int32 [8], P('dom'), may hold values from 1 to 1536, 6144 in all
Outputs:
- node_grad: bfloat16 [2048, 512], P('dom', 'tensor')
- w_in_grad: float32 [512, 1024], P('tensor')
- w_out_grad: float32 [512, 512], P('tensor')
The draws below stay inside these ranges and needn't reach their ends.
Inputs may be any that keep to these rules, and one draw needn't show every extreme that they name: `edge_count`: live slots of a partition come first; some partition has all 1536 live.
All inputs are finite; a program needn't handle non-finite values. No bound on the sum of `edge_count` on one device may be relied on, other than what follows from the above.
Results may differ from the reference program's by a relative error of at most 0.0049.
Values may be sent and summed in bfloat16 or wider, within the bound.
A program may use at most 64 MiB of HBM per device.

```python
import math
import jax
import jax.numpy as jnp
import numpy as np
from jax import lax

D = 512
H = 512
NODE_DEV = 256
E_DEV = 1536
NBR = 7
CAP = 16
NODES = 2048
EDGES = 12288
TABLE = 368
N_DOM = 8


def touch_ends(values, own_key, low, high):
    longest = values.shape.index(max(values.shape))
    spots = []
    for shift in (0, 1):
        where = [jax.random.randint(jax.random.fold_in(own_key, axis), (), 0, length) for axis, length in enumerate(values.shape)]
        where[longest] = (where[longest] + shift) % values.shape[longest]
        spots.append(tuple(where))
    return values.at[spots[0]].set(low).at[spots[1]].set(high)


def block_levels(stream_key, shape, split, least, high):
    loudness = 1.0
    for axis_at, blocks in split:
        heights = jax.random.uniform(jax.random.fold_in(jax.random.fold_in(stream_key, 6), axis_at), (blocks,), jnp.float32, least / len(split), high / len(split))
        loudness = loudness * jnp.repeat(jnp.exp(heights), shape[axis_at] // blocks).reshape((-1,) + (1,) * (len(shape) - 1 - axis_at))
    return loudness


def length_profile(count, total, reach, skew):
    portions = [(1 << 20) // math.isqrt(grade ** skew) + 1 for grade in range(2, count + 1)]
    rest, holding = total - reach - (count - 1), [1] * (count - 1)
    while rest > 0:
        movable = [i for i in range(count - 1) if holding[i] < reach]
        mass, remaining = sum([portions[i] for i in movable]), rest
        for i in movable:
            addition = min(reach - holding[i], max(1, remaining * portions[i] // mass), rest)
            holding[i] = holding[i] + addition
            rest = rest - addition
    return np.array([reach] + holding)


def ragged_sizes(key, count, total, limit, lean):
    if count == 2:
        one = jax.random.randint(key, (), max(1, total - limit), min(limit, total - 1) + 1)
        return jnp.stack([one, total - one])
    sizes = jnp.asarray(length_profile(count, total, limit, lean), jnp.int32)
    couples = (count - 1) // 2
    giver, taker = sizes[1:1 + 2 * couples:2], sizes[2:2 + 2 * couples:2]
    room = jnp.minimum(giver - 1, limit - taker)
    shifted = jax.random.randint(jax.random.fold_in(key, 1), (couples,), 0, 1 << 20) % (room + 1)
    sizes = sizes.at[1:1 + 2 * couples:2].set(giver - shifted).at[2:2 + 2 * couples:2].set(taker + shifted)
    return sizes[jax.random.permutation(jax.random.fold_in(key, 2), count)]


def normal_values(own_key, dims, spread, limit, shards=(), kind=jnp.bfloat16):
    values = jax.random.normal(own_key, dims, jnp.float32) * spread
    if len(shards) > 0:
        values = block_levels(own_key, dims, shards, -0.22, 0.18) * values
    return jnp.clip(values, min=-limit, max=limit).astype(kind)


def setup_inputs(seed: int = 0) -> dict:
    splits = jax.random.split(jax.random.key(seed), 9)
    return {
        "node_state": normal_values(splits[0], (NODES, D), 1.0, 6.0, ((0, 8), (1, 4))),
        "cotangent": normal_values(splits[1], (NODES, D), 1.0, 6.0, ((0, 8), (1, 4))),
        "w_in": normal_values(splits[2], (H, 2 * D), (2 * D) ** -0.5, 0.1875, ((0, 4),)),
        "w_out": normal_values(splits[3], (H, D), H ** -0.5, 0.25, ((0, 4),)),
        "send_list": touch_ends(jax.random.randint(splits[4], (N_DOM, NBR, CAP), 0, NODE_DEV), jax.random.fold_in(splits[4], 1), 0, NODE_DEV - 1).astype(jnp.int32),
        "sender": touch_ends(jax.random.randint(splits[5], (EDGES,), 0, TABLE), jax.random.fold_in(splits[5], 1), 0, TABLE - 1).astype(jnp.int32),
        "receiver": touch_ends(jax.random.randint(splits[6], (EDGES,), 0, NODE_DEV), jax.random.fold_in(splits[6], 1), 0, NODE_DEV - 1).astype(jnp.int32),
        "edge_count": ragged_sizes(splits[7], N_DOM, N_DOM * E_DEV // 2, E_DEV, 2).astype(jnp.int32),
    }


def silu_parts(pre):
    sig = jax.nn.sigmoid(pre)
    return pre * sig, sig * (1.0 + pre * (1.0 - sig))


def neighbour_offsets(count):
    return [1, count - 1, 2, count - 2, 3, count - 3, count // 2]


def reference(node_state, cotangent, w_in, w_out, send_list, sender, receiver, edge_count):
    blocks = node_state.reshape(N_DOM, NODE_DEV, D)
    cot_blocks = cotangent.reshape(N_DOM, NODE_DEV, D)
    offsets = jnp.array(neighbour_offsets(N_DOM), dtype=jnp.int32)
    parts = jnp.arange(N_DOM, dtype=jnp.int32)
    slot_ids = jnp.arange(NBR, dtype=jnp.int32)
    source = (parts[:, None] - offsets[None, :]) % N_DOM
    target = (parts[:, None] + offsets[None, :]) % N_DOM
    picked = send_list[source, slot_ids[None, :]]
    halo = blocks[source[:, :, None], picked].reshape(N_DOM, NBR * CAP, D)
    senders = sender.reshape(N_DOM, E_DEV)
    receivers = receiver.reshape(N_DOM, E_DEV)
    w_send = w_in[:, :D]
    w_recv = w_in[:, D:]

    def one_part(items):
        local, incoming, cot, send_idx, recv_idx, count = items
        table = jnp.concatenate([local, incoming], 0)
        sent = table[send_idx]
        recv = local[recv_idx]
        pre = jnp.dot(sent, w_send.T, preferred_element_type=jnp.float32) + jnp.dot(recv, w_recv.T, preferred_element_type=jnp.float32)
        act, slope = silu_parts(pre)
        act = act.astype(jnp.bfloat16)
        live = (jnp.arange(E_DEV, dtype=jnp.int32) < count).astype(jnp.bfloat16)
        message_grad = cot[recv_idx] * live[:, None]
        out_grad = jnp.dot(act.T, message_grad, preferred_element_type=jnp.float32)
        hidden_grad = jnp.dot(message_grad, w_out.T, preferred_element_type=jnp.float32)
        pre_grad = (hidden_grad * slope).astype(jnp.bfloat16)
        in_grad = jnp.concatenate([jnp.dot(pre_grad.T, sent, preferred_element_type=jnp.float32), jnp.dot(pre_grad.T, recv, preferred_element_type=jnp.float32)], 1)
        send_sum = jax.ops.segment_sum(pre_grad.astype(jnp.float32), send_idx, TABLE).astype(jnp.bfloat16)
        recv_sum = jax.ops.segment_sum(pre_grad.astype(jnp.float32), recv_idx, NODE_DEV).astype(jnp.bfloat16)
        row_grad = jnp.dot(send_sum, w_send, preferred_element_type=jnp.float32)
        row_grad = row_grad.at[:NODE_DEV].add(jnp.dot(recv_sum, w_recv, preferred_element_type=jnp.float32))
        return row_grad, in_grad, out_grad

    row_grad, in_grad, out_grad = lax.map(one_part, (blocks, halo, cot_blocks, senders, receivers, edge_count))
    halo_grad = row_grad[:, NODE_DEV:].reshape(N_DOM, NBR, CAP, D)
    back = halo_grad[target, slot_ids[None, :]]

    def owner_sum(values, index):
        return jax.ops.segment_sum(values.reshape(-1, D), index.reshape(-1), NODE_DEV)

    extra = jax.vmap(owner_sum)(back, send_list)
    node_grad = cot_blocks.astype(jnp.float32) + row_grad[:, :NODE_DEV] + extra
    scale = EDGES ** -0.5
    return node_grad.reshape(NODES, D).astype(jnp.bfloat16), jnp.sum(in_grad, 0) * scale, jnp.sum(out_grad, 0) * scale
```

```python
import functools

import jax
import jax.numpy as jnp
from jax import lax
from jax.experimental import pallas as pl
from jax.experimental.pallas import tpu as pltpu
from jax.sharding import PartitionSpec as P


def shifted(value, axis, steps):
    count = lax.axis_size(axis)
    pairs = [(source, (source + steps) % count) for source in range(count)]
    return lax.ppermute(value, axis, pairs)


def contract_rows(left, right):
    return lax.dot_general(
        left, right, (((0,), (0,)), ((), ())), preferred_element_type=jnp.float32
    )


def contract_cols(left, right):
    return lax.dot_general(
        left, right, (((1,), (1,)), ((), ())), preferred_element_type=jnp.float32
    )


def neighbour_offsets(count):
    return [1, count - 1, 2, count - 2, 3, count - 3, count // 2]


def per_device(node_state, cotangent, w_in, w_out, send_list, sender, receiver, edge_count):
    local_rows = node_state.shape[0]
    slots = send_list.shape[2]
    peers = send_list.shape[1]
    parts = lax.axis_size("dom")
    offsets = neighbour_offsets(parts)
    my_list = send_list[0]
    arrived = []
    for which, offset in enumerate(offsets):
        arrived.append(shifted(node_state[my_list[which]], "dom", offset))
    incoming = jnp.concatenate(arrived, 0)
    table_part = jnp.concatenate([node_state, incoming], 0)
    table, cot_full = (
        lax.all_gather(table_part, "tensor", axis=1, tiled=True),
        lax.all_gather(cotangent, "tensor", axis=1, tiled=True),
    )
    width = table.shape[1]
    rows = table.shape[0]
    w_send = w_in[:, :width]
    w_recv = w_in[:, width:]
    sent = table[sender]
    recv = table[receiver]
    pre = contract_cols(sent, w_send) + contract_cols(recv, w_recv)
    sig = jax.nn.sigmoid(pre)
    act = (pre * sig).astype(jnp.bfloat16)
    slope = sig * (1.0 + pre * (1.0 - sig))
    live = (jnp.arange(sender.shape[0], dtype=jnp.int32) < edge_count[0]).astype(jnp.bfloat16)
    message_grad = cot_full[receiver] * live[:, None]
    out_grad = contract_rows(act, message_grad)
    hidden_grad = contract_cols(message_grad, w_out)
    pre_grad = (hidden_grad * slope).astype(jnp.bfloat16)
    in_grad = jnp.concatenate([contract_rows(pre_grad, sent), contract_rows(pre_grad, recv)], 1)
    hit_send = (sender[:, None] == jnp.arange(rows, dtype=jnp.int32)[None, :]).astype(jnp.bfloat16)
    hit_recv = (receiver[:, None] == jnp.arange(local_rows, dtype=jnp.int32)[None, :]).astype(
        jnp.bfloat16
    )
    send_sum = contract_rows(hit_send, pre_grad).astype(jnp.bfloat16)
    recv_sum = contract_rows(hit_recv, pre_grad).astype(jnp.bfloat16)
    term = jnp.dot(send_sum, w_send, preferred_element_type=jnp.float32)
    term = term.at[:local_rows].add(jnp.dot(recv_sum, w_recv, preferred_element_type=jnp.float32))
    row_grad = lax.psum_scatter(term, "tensor", scatter_dimension=1, tiled=True)
    feat_part = row_grad.shape[1]
    halo_grad = row_grad[local_rows:].reshape(peers, slots, feat_part)
    node_grad = cotangent.astype(jnp.float32) + row_grad[:local_rows]
    for which, offset in enumerate(offsets):
        returned = shifted(halo_grad[which], "dom", parts - offset)
        node_grad = node_grad.at[my_list[which]].add(returned)
    sum_in, sum_out = lax.psum((in_grad, out_grad), "dom")
    scale = float(sender.shape[0] * parts) ** (-0.5)
    return (node_grad.astype(jnp.bfloat16), sum_in * scale, sum_out * scale)


MESH = pl.DeviceIdType.MESH


def dot(left, right):
    return jnp.dot(left, right, preferred_element_type=jnp.float32)


def split(value):
    high = value.astype(jnp.bfloat16)
    low = (value - high.astype(jnp.float32)).astype(jnp.bfloat16)
    return jnp.concatenate([high, low], 0)


def layer_kernel(
    parts, tps, offsets, slots, scale,
    x_ref, c_ref, win_ref, wout_ref, list_ref, send_ref, recv_ref, count_ref,
    node_ref, gin_ref, gout_ref,
    xf, cf, st_loc, st_hal, rt, lt, ap, pre_buf, hid_buf,
    halo_out, halo_in, back_out, back_in, sums, rs, ag_out, ag, part_f, part_b, part_in,
    gx_s, gx_r, gc_s, gc_r, h_s, h_r, b_s, b_r, rs_s, rs_r, ag_s, ag_r, p_s, p_r,
):
    me = lax.axis_index("dom")
    mt = lax.axis_index("tensor")
    rows, feat = x_ref.shape
    hid = win_ref.shape[0]
    width = feat * tps
    edges = send_ref.shape[1]
    peers = len(offsets)
    halos = peers * slots
    chunk = hid // parts
    tile = 512 if edges % 512 == 0 else edges
    tiles = [slice(i, i + tile) for i in range(0, edges, tile)]

    def mod(value, count):
        return lax.rem(value + count, count)

    def copy(src, dst, ss, rsem, **where):
        return pltpu.make_async_remote_copy(
            src_ref=src, dst_ref=dst, send_sem=ss, recv_sem=rsem,
            device_id=where, device_id_type=MESH,
        )

    barrier = pltpu.get_barrier_semaphore()
    for k in range(1, tps):
        pl.semaphore_signal(barrier, inc=1, device_id={"tensor": mod(mt + k, tps)}, device_id_type=MESH)
    for k in range(1, parts):
        pl.semaphore_signal(barrier, inc=1, device_id={"dom": mod(me + k, parts)}, device_id_type=MESH)
    pl.semaphore_wait(barrier, tps - 1 + parts - 1)

    mine = pl.ds(pl.multiple_of(mt * feat, feat), feat)
    x_copies = [
        copy(x_ref, xf.at[:, mine], gx_s.at[k], gx_r.at[k], tensor=mod(mt + k, tps))
        for k in range(1, tps)
    ]
    c_copies = [
        copy(c_ref, cf.at[:, mine], gc_s.at[k], gc_r.at[k], tensor=mod(mt + k, tps))
        for k in range(1, tps)
    ]
    for item in x_copies + c_copies:
        item.start()
    xf[:, mine] = x_ref[...]
    cf[:, mine] = c_ref[...]

    def hits(index, first, count):
        lanes = index.shape[1]
        spot = lax.broadcasted_iota(jnp.int32, (count, lanes), 0) + first
        return jnp.where(spot == index, 1.0, 0.0).astype(jnp.bfloat16)

    lt[...] = hits(list_ref[...], 0, rows)
    count = count_ref[0]
    for cols in tiles:
        where = lax.broadcasted_iota(jnp.int32, (1, tile), 1) + cols.start
        target = jnp.where(where < count, recv_ref[:, cols], -1)
        rt[:, cols] = hits(target, 0, rows)
        st_loc[:, cols] = hits(send_ref[:, cols], 0, rows)
        st_hal[:, cols] = hits(send_ref[:, cols], rows, halos)

    for item in x_copies:
        item.wait_recv()
    own = split(contract_cols(win_ref[:, :width], xf[...]))
    picked = dot(own, lt[...])
    halo_out[...] = (picked[:hid] + picked[hid:]).T
    h_copies = []
    for j, offset in enumerate(offsets):
        band = slice(j * slots, (j + 1) * slots)
        item = copy(
            halo_out.at[band], halo_in.at[band], h_s.at[j], h_r.at[j],
            dom=mod(me + offset, parts),
        )
        item.start()
        h_copies.append(item)

    at_recv = split(contract_cols(win_ref[:, width:], xf[...]))
    for cols in tiles:
        both = dot(own, st_loc[:, cols]) + dot(at_recv, rt[:, cols])
        pre_buf[:, cols] = both[:hid] + both[hid:]
    for item in c_copies:
        item.wait_recv()
    grad = split(contract_cols(wout_ref[...], cf[...]))
    for cols in tiles:
        both = dot(grad, rt[:, cols])
        hid_buf[:, cols] = both[:hid] + both[hid:]

    for item in h_copies:
        item.wait_recv()
    far = split(halo_in[...].T)
    for cols in tiles:
        both = dot(far, st_hal[:, cols])
        pre = pre_buf[:, cols] + both[:hid] + both[hid:]
        sig = jax.nn.sigmoid(pre)
        slope = sig * (1.0 + pre * (1.0 - sig))
        ap[:hid, cols] = (pre * sig).astype(jnp.bfloat16)
        ap[hid:, cols] = (hid_buf[:, cols] * slope).astype(jnp.bfloat16)

    back_out[...] = contract_cols(st_hal[...], ap[hid:]).astype(jnp.bfloat16)
    b_copies = []
    for j, offset in enumerate(offsets):
        band = slice(j * slots, (j + 1) * slots)
        item = copy(
            back_out.at[band], back_in.at[band], b_s.at[j], b_r.at[j],
            dom=mod(me - offset, parts),
        )
        item.start()
        b_copies.append(item)

    spans = [slice(width, 3 * width), slice(0, width)]

    def scatter(which):
        out = []
        for k in range(1, parts):
            peer = mod(me + k, parts)
            band = pl.ds(pl.multiple_of(peer * chunk, chunk), chunk)
            item = copy(
                sums.at[band, spans[which]], rs.at[k, :, spans[which]],
                rs_s.at[which, k], rs_r.at[which, k], dom=peer,
            )
            item.start()
            out.append(item)
        return out

    ours = pl.ds(pl.multiple_of(me * chunk, chunk), chunk)

    def reduce(which, arrivals):
        span = spans[which]
        total = sums[ours, span].astype(jnp.float32)
        for k, item in enumerate(arrivals):
            item.wait_recv()
            total = total + rs[k + 1, :, span].astype(jnp.float32)
        total = total.astype(jnp.bfloat16)
        ag_out[:, span] = total
        ag[ours, span] = total
        out = []
        for k in range(1, parts):
            item = copy(
                ag_out.at[:, span], ag.at[ours, span],
                ag_s.at[which, k], ag_r.at[which, k], dom=mod(me + k, parts),
            )
            item.start()
            out.append(item)
        return out

    at_node = contract_cols(ap[...], rt[...])
    act_sum = at_node[:hid].astype(jnp.bfloat16)
    recv_sum = at_node[hid:].astype(jnp.bfloat16)
    sums[:, 2 * width:] = dot(act_sum, cf[...]).astype(jnp.bfloat16)
    sums[:, width:2 * width] = dot(recv_sum, xf[...]).astype(jnp.bfloat16)
    first = scatter(0)
    near = contract_cols(ap[hid:], st_loc[...])
    part_f[...] = dot(at_node[hid:].T.astype(jnp.bfloat16), win_ref[:, width:])

    for item in b_copies:
        item.wait_recv()
    returned = back_in[...].astype(jnp.float32).T.astype(jnp.bfloat16)
    whole = near + contract_cols(returned, lt[...])
    sums[:, :width] = dot(whole.astype(jnp.bfloat16), xf[...]).astype(jnp.bfloat16)
    second = scatter(1)
    share = part_f[...] + dot(whole.T.astype(jnp.bfloat16), win_ref[:, :width])
    part_f[...] = share
    part_b[...] = share.astype(jnp.bfloat16)
    p_copies = []
    for k in range(1, tps):
        peer = mod(mt + k, tps)
        theirs = pl.ds(pl.multiple_of(peer * feat, feat), feat)
        item = copy(part_b.at[:, theirs], part_in.at[k], p_s.at[k], p_r.at[k], tensor=peer)
        item.start()
        p_copies.append(item)

    gathers = reduce(0, first)
    node = c_ref[...].astype(jnp.float32) + part_f[:, mine]
    for k, item in enumerate(p_copies):
        item.wait_recv()
        node = node + part_in[k + 1].astype(jnp.float32)
    node_ref[...] = node.astype(jnp.bfloat16)
    gathers += reduce(1, second)
    for item in gathers:
        item.wait_recv()
    gin_ref[...] = ag[:, :2 * width].astype(jnp.float32) * scale
    gout_ref[...] = ag[:, 2 * width:].astype(jnp.float32) * scale
    for item in x_copies + c_copies + h_copies + b_copies + first + second + p_copies + gathers:
        item.wait_send()


def fused(node_state, cotangent, w_in, w_out, send_list, sender, receiver, edge_count):
    parts = lax.axis_size("dom")
    tps = lax.axis_size("tensor")
    rows, feat = node_state.shape
    hid = w_in.shape[0]
    width = feat * tps
    edges = sender.shape[0]
    _, peers, slots = send_list.shape
    halos = peers * slots
    offsets = neighbour_offsets(parts)
    chunk = hid // parts
    scale = float(edges * parts) ** (-0.5)
    bf16, f32 = jnp.bfloat16, jnp.float32
    vm, dma = pltpu.VMEM, pltpu.SemaphoreType.DMA
    spec = pl.BlockSpec(memory_space=pltpu.VMEM)
    return pl.pallas_call(
        functools.partial(layer_kernel, parts, tps, offsets, slots, scale),
        out_shape=(
            jax.ShapeDtypeStruct((rows, feat), bf16),
            jax.ShapeDtypeStruct((hid, 2 * width), f32),
            jax.ShapeDtypeStruct((hid, width), f32),
        ),
        in_specs=[spec] * 7 + [pl.BlockSpec(memory_space=pltpu.SMEM)],
        out_specs=(spec, spec, spec),
        scratch_shapes=[
            vm((rows, width), bf16),
            vm((rows, width), bf16),
            vm((rows, edges), bf16),
            vm((halos, edges), bf16),
            vm((rows, edges), bf16),
            vm((rows, halos), bf16),
            vm((2 * hid, edges), bf16),
            vm((hid, edges), f32),
            vm((hid, edges), f32),
            vm((halos, hid), f32),
            vm((halos, hid), f32),
            vm((halos, hid), bf16),
            vm((halos, hid), bf16),
            vm((hid, 3 * width), bf16),
            vm((parts, chunk, 3 * width), bf16),
            vm((chunk, 3 * width), bf16),
            vm((hid, 3 * width), bf16),
            vm((rows, width), f32),
            vm((rows, width), bf16),
            vm((tps, rows, feat), bf16),
            dma((tps,)), dma((tps,)), dma((tps,)), dma((tps,)),
            dma((peers,)), dma((peers,)), dma((peers,)), dma((peers,)),
            dma((2, parts)), dma((2, parts)), dma((2, parts)), dma((2, parts)),
            dma((tps,)), dma((tps,)),
        ],
        compiler_params=pltpu.CompilerParams(
            collective_id=0, has_side_effects=True, vmem_limit_bytes=48 * 1024 * 1024
        ),
    )(
        node_state, cotangent, w_in, w_out, send_list.reshape(1, halos),
        sender.reshape(1, edges), receiver.reshape(1, edges), edge_count,
    )


def layer(node_state, cotangent, w_in, w_out, send_list, sender, receiver, edge_count):
    parts = lax.axis_size("dom")
    fits = (
        node_state.shape[1] % 128 == 0
        and node_state.shape[0] % 16 == 0
        and send_list.shape[2] % 16 == 0
        and w_in.shape[0] % (16 * parts) == 0
        and sender.shape[0] % 128 == 0
    )
    plan = fused if fits else per_device
    return plan(node_state, cotangent, w_in, w_out, send_list, sender, receiver, edge_count)


def solution(mesh):
    return jax.shard_map(
        layer,
        mesh=mesh,
        in_specs=(
            P("dom", "tensor"),
            P("dom", "tensor"),
            P("tensor", None),
            P("tensor", None),
            P("dom", None, None),
            P("dom"),
            P("dom"),
            P("dom"),
        ),
        out_specs=(P("dom", "tensor"), P("tensor", None), P("tensor", None)),
        check_vma=False,
    )
```

```python
import functools

import jax
import jax.numpy as jnp
from jax import lax
from jax.experimental import pallas as pl
from jax.experimental.pallas import tpu as pltpu
from jax.sharding import PartitionSpec as P


def shifted(value, axis, steps):
    count = lax.axis_size(axis)
    pairs = [(source, (source + steps) % count) for source in range(count)]
    return lax.ppermute(value, axis, pairs)


def contract_rows(left, right):
    return lax.dot_general(
        left, right, (((0,), (0,)), ((), ())), preferred_element_type=jnp.float32
    )


def contract_cols(left, right):
    return lax.dot_general(
        left, right, (((1,), (1,)), ((), ())), preferred_element_type=jnp.float32
    )


def neighbour_offsets(count):
    return [1, count - 1, 2, count - 2, 3, count - 3, count // 2]


def per_device(node_state, cotangent, w_in, w_out, send_list, sender, receiver, edge_count):
    local_rows = node_state.shape[0]
    slots = send_list.shape[2]
    peers = send_list.shape[1]
    parts = lax.axis_size("dom")
    offsets = neighbour_offsets(parts)
    my_list = send_list[0]
    arrived = []
    for which, offset in enumerate(offsets):
        arrived.append(shifted(node_state[my_list[which]], "dom", offset))
    incoming = jnp.concatenate(arrived, 0)
    table_part = jnp.concatenate([node_state, incoming], 0)
    table, cot_full = (
        lax.all_gather(table_part, "tensor", axis=1, tiled=True),
        lax.all_gather(cotangent, "tensor", axis=1, tiled=True),
    )
    width = table.shape[1]
    rows = table.shape[0]
    w_send = w_in[:, :width]
    w_recv = w_in[:, width:]
    sent = table[sender]
    recv = table[receiver]
    pre = contract_cols(sent, w_send) + contract_cols(recv, w_recv)
    sig = jax.nn.sigmoid(pre)
    act = (pre * sig).astype(jnp.bfloat16)
    slope = sig * (1.0 + pre * (1.0 - sig))
    live = (jnp.arange(sender.shape[0], dtype=jnp.int32) < edge_count[0]).astype(jnp.bfloat16)
    message_grad = cot_full[receiver] * live[:, None]
    out_grad = contract_rows(act, message_grad)
    hidden_grad = contract_cols(message_grad, w_out)
    pre_grad = (hidden_grad * slope).astype(jnp.bfloat16)
    in_grad = jnp.concatenate([contract_rows(pre_grad, sent), contract_rows(pre_grad, recv)], 1)
    hit_send = (sender[:, None] == jnp.arange(rows, dtype=jnp.int32)[None, :]).astype(jnp.bfloat16)
    hit_recv = (receiver[:, None] == jnp.arange(local_rows, dtype=jnp.int32)[None, :]).astype(
        jnp.bfloat16
    )
    send_sum = contract_rows(hit_send, pre_grad).astype(jnp.bfloat16)
    recv_sum = contract_rows(hit_recv, pre_grad).astype(jnp.bfloat16)
    term = jnp.dot(send_sum, w_send, preferred_element_type=jnp.float32)
    term = term.at[:local_rows].add(jnp.dot(recv_sum, w_recv, preferred_element_type=jnp.float32))
    row_grad = lax.psum_scatter(term, "tensor", scatter_dimension=1, tiled=True)
    feat_part = row_grad.shape[1]
    halo_grad = row_grad[local_rows:].reshape(peers, slots, feat_part)
    node_grad = cotangent.astype(jnp.float32) + row_grad[:local_rows]
    for which, offset in enumerate(offsets):
        returned = shifted(halo_grad[which], "dom", parts - offset)
        node_grad = node_grad.at[my_list[which]].add(returned)
    sum_in, sum_out = lax.psum((in_grad, out_grad), "dom")
    scale = float(sender.shape[0] * parts) ** (-0.5)
    return (node_grad.astype(jnp.bfloat16), sum_in * scale, sum_out * scale)


MESH = pl.DeviceIdType.MESH


def dot(left, right):
    return jnp.dot(left, right, preferred_element_type=jnp.float32)


def split(value):
    high = value.astype(jnp.bfloat16)
    low = (value - high.astype(jnp.float32)).astype(jnp.bfloat16)
    return jnp.concatenate([high, low], 0)


def layer_kernel(
    parts, tps, offsets, slots,
    x_ref, c_ref, win_any, wout_any, list_any, send_any, recv_any, count_ref,
    node_ref, ag_ref,
    win_ref, wout_ref, list_ref, send_ref, recv_ref, spot_ref, load_s, xf, cf, st_loc, st_hal, rt, lt, ap, pre_buf, hid_buf,
    halo_out, halo_in, back_out, back_in, sums, rs, ag_out, ag, part_f, part_b, part_in,
    gx_s, gx_r, gc_s, gc_r, h_s, h_r, b_s, b_r, rs_s, rs_r, ag_s, ag_r, p_s, p_r,
):
    me = lax.axis_index("dom")
    mt = lax.axis_index("tensor")
    rows, feat = x_ref.shape
    hid = win_ref.shape[0]
    width = feat * tps
    edges = send_ref.shape[0]
    peers = len(offsets)
    halos = peers * slots
    chunk = hid // parts
    tile = 512 if edges % 512 == 0 else edges
    tiles = [slice(i, i + tile) for i in range(0, edges, tile)]

    def mod(value, count):
        return lax.rem(value + count, count)

    def copy(src, dst, ss, rsem, **where):
        return pltpu.make_async_remote_copy(
            src_ref=src, dst_ref=dst, send_sem=ss, recv_sem=rsem,
            device_id=where, device_id_type=MESH,
        )

    barrier = pltpu.get_barrier_semaphore()
    for k in range(1, tps):
        pl.semaphore_signal(barrier, inc=1, device_id={"tensor": mod(mt + k, tps)}, device_id_type=MESH)
    for k in range(1, parts):
        pl.semaphore_signal(barrier, inc=1, device_id={"dom": mod(me + k, parts)}, device_id_type=MESH)

    mine = pl.ds(pl.multiple_of(mt * feat, feat), feat)
    pairs = [
        (list_any, list_ref), (send_any, send_ref), (recv_any, recv_ref),
        (x_ref, xf.at[:, mine]), (win_any, win_ref), (c_ref, cf.at[:, mine]), (wout_any, wout_ref),
    ]
    loads = [pltpu.make_async_copy(a, b, load_s.at[i]) for i, (a, b) in enumerate(pairs)]
    for item in loads:
        item.start()
    pl.semaphore_wait(barrier, tps - 1 + parts - 1)

    x_copies = [
        copy(x_ref, xf.at[:, mine], gx_s.at[k], gx_r.at[k], tensor=mod(mt + k, tps))
        for k in range(1, tps)
    ]
    c_copies = [
        copy(c_ref, cf.at[:, mine], gc_s.at[k], gc_r.at[k], tensor=mod(mt + k, tps))
        for k in range(1, tps)
    ]
    for item in x_copies + c_copies:
        item.start()

    def hits(index, first, count):
        lanes = index.shape[1]
        spot = lax.broadcasted_iota(jnp.int32, (count, lanes), 0) + first
        return jnp.where(spot == index, 1.0, 0.0).astype(jnp.bfloat16)

    for item in loads[:3]:
        item.wait()
    for j in range(peers):
        spot_ref[:, j * slots:(j + 1) * slots] = list_ref[j]
    lt[...] = hits(spot_ref[...], 0, rows)
    count = count_ref[0]
    for cols in tiles:
        where = lax.broadcasted_iota(jnp.int32, (1, tile), 1) + cols.start
        target = jnp.where(where < count, recv_ref[cols].reshape(1, tile), -1)
        rt[:, cols] = hits(target, 0, rows)
        sends = send_ref[cols].reshape(1, tile)
        st_loc[:, cols] = hits(sends, 0, rows)
        st_hal[:, cols] = hits(sends, rows, halos)

    for item in loads[3:5]:
        item.wait()
    for item in x_copies:
        item.wait_recv()
    own = split(contract_cols(win_ref[:, :width], xf[...]))
    picked = dot(own, lt[...])
    halo_out[...] = (picked[:hid] + picked[hid:]).T
    h_copies = []
    for j, offset in enumerate(offsets):
        band = slice(j * slots, (j + 1) * slots)
        item = copy(
            halo_out.at[band], halo_in.at[band], h_s.at[j], h_r.at[j],
            dom=mod(me + offset, parts),
        )
        item.start()
        h_copies.append(item)

    at_recv = split(contract_cols(win_ref[:, width:], xf[...]))
    for cols in tiles:
        both = dot(own, st_loc[:, cols]) + dot(at_recv, rt[:, cols])
        pre_buf[:, cols] = both[:hid] + both[hid:]
    for item in loads[5:]:
        item.wait()
    for item in c_copies:
        item.wait_recv()
    grad = split(contract_cols(wout_ref[...], cf[...]))
    for cols in tiles:
        both = dot(grad, rt[:, cols])
        hid_buf[:, cols] = both[:hid] + both[hid:]

    for item in h_copies:
        item.wait_recv()
    far = split(halo_in[...].T)
    for cols in tiles:
        both = dot(far, st_hal[:, cols])
        pre = pre_buf[:, cols] + both[:hid] + both[hid:]
        sig = jax.nn.sigmoid(pre)
        slope = sig * (1.0 + pre * (1.0 - sig))
        ap[:hid, cols] = (pre * sig).astype(jnp.bfloat16)
        ap[hid:, cols] = (hid_buf[:, cols] * slope).astype(jnp.bfloat16)

    back_out[...] = contract_cols(st_hal[...], ap[hid:]).astype(jnp.bfloat16)
    b_copies = []
    for j, offset in enumerate(offsets):
        band = slice(j * slots, (j + 1) * slots)
        item = copy(
            back_out.at[band], back_in.at[band], b_s.at[j], b_r.at[j],
            dom=mod(me - offset, parts),
        )
        item.start()
        b_copies.append(item)

    spans = [slice(width, 3 * width), slice(0, width)]

    def scatter(which):
        out = []
        for k in range(1, parts):
            peer = mod(me + k, parts)
            band = pl.ds(pl.multiple_of(peer * chunk, chunk), chunk)
            item = copy(
                sums.at[band, spans[which]], rs.at[k, :, spans[which]],
                rs_s.at[which, k], rs_r.at[which, k], dom=peer,
            )
            item.start()
            out.append(item)
        return out

    ours = pl.ds(pl.multiple_of(me * chunk, chunk), chunk)

    def reduce(which, arrivals):
        span = spans[which]
        total = sums[ours, span].astype(jnp.float32)
        for k, item in enumerate(arrivals):
            item.wait_recv()
            total = total + rs[k + 1, :, span].astype(jnp.float32)
        total = total.astype(jnp.bfloat16)
        ag_out[:, span] = total
        ag[ours, span] = total
        out = []
        for k in range(1, parts):
            item = copy(
                ag_out.at[:, span], ag.at[ours, span],
                ag_s.at[which, k], ag_r.at[which, k], dom=mod(me + k, parts),
            )
            item.start()
            out.append(item)
        return out

    at_node = contract_cols(ap[...], rt[...])
    act_sum = at_node[:hid].astype(jnp.bfloat16)
    recv_sum = at_node[hid:].astype(jnp.bfloat16)
    sums[:, 2 * width:] = dot(act_sum, cf[...]).astype(jnp.bfloat16)
    sums[:, width:2 * width] = dot(recv_sum, xf[...]).astype(jnp.bfloat16)
    first = scatter(0)
    near = contract_cols(ap[hid:], st_loc[...])
    part_f[...] = dot(at_node[hid:].T.astype(jnp.bfloat16), win_ref[:, width:])

    for item in b_copies:
        item.wait_recv()
    returned = back_in[...].astype(jnp.float32).T.astype(jnp.bfloat16)
    whole = near + contract_cols(returned, lt[...])
    sums[:, :width] = dot(whole.astype(jnp.bfloat16), xf[...]).astype(jnp.bfloat16)
    second = scatter(1)
    share = part_f[...] + dot(whole.T.astype(jnp.bfloat16), win_ref[:, :width])
    part_f[...] = share
    part_b[...] = share.astype(jnp.bfloat16)
    p_copies = []
    for k in range(1, tps):
        peer = mod(mt + k, tps)
        theirs = pl.ds(pl.multiple_of(peer * feat, feat), feat)
        item = copy(part_b.at[:, theirs], part_in.at[k], p_s.at[k], p_r.at[k], tensor=peer)
        item.start()
        p_copies.append(item)

    gathers = reduce(0, first)
    node = cf[:, mine].astype(jnp.float32) + part_f[:, mine]
    for k, item in enumerate(p_copies):
        item.wait_recv()
        node = node + part_in[k + 1].astype(jnp.float32)
    node_ref[...] = node.astype(jnp.bfloat16)
    gathers += reduce(1, second)
    for item in gathers:
        item.wait_recv()
    ag_ref[...] = ag[...]
    for item in x_copies + c_copies + h_copies + b_copies + first + second + p_copies + gathers:
        item.wait_send()


def write_kernel(scale, node_ref, ag_ref, node_any, gin_any, gout_any, gin_ref, gout_ref, sems):
    cut = gin_ref.shape[1]
    node_copy = pltpu.make_async_copy(node_ref, node_any, sems.at[0])
    node_copy.start()
    gin_ref[...] = ag_ref[:, :cut].astype(jnp.float32) * scale
    gin_copy = pltpu.make_async_copy(gin_ref, gin_any, sems.at[1])
    gin_copy.start()
    gout_ref[...] = ag_ref[:, cut:].astype(jnp.float32) * scale
    gout_copy = pltpu.make_async_copy(gout_ref, gout_any, sems.at[2])
    gout_copy.start()
    node_copy.wait()
    gin_copy.wait()
    gout_copy.wait()


def fused(node_state, cotangent, w_in, w_out, send_list, sender, receiver, edge_count):
    parts = lax.axis_size("dom")
    tps = lax.axis_size("tensor")
    rows, feat = node_state.shape
    hid = w_in.shape[0]
    width = feat * tps
    edges = sender.shape[0]
    _, peers, slots = send_list.shape
    halos = peers * slots
    offsets = neighbour_offsets(parts)
    chunk = hid // parts
    scale = float(edges * parts) ** (-0.5)
    bf16, f32 = jnp.bfloat16, jnp.float32
    vm, dma = pltpu.VMEM, pltpu.SemaphoreType.DMA
    spec = pl.BlockSpec(memory_space=pltpu.VMEM)
    hbm = pl.BlockSpec(memory_space=pltpu.HBM)
    operands = [
        pltpu.with_memory_space_constraint(item, pltpu.HBM)
        for item in (
            node_state, cotangent, w_in, w_out, send_list.transpose(1, 0, 2),
            sender, receiver,
        )
    ]
    node, total = pl.pallas_call(
        functools.partial(layer_kernel, parts, tps, offsets, slots),
        out_shape=(
            jax.ShapeDtypeStruct((rows, feat), bf16),
            jax.ShapeDtypeStruct((hid, 3 * width), bf16),
        ),
        in_specs=[hbm] * 7 + [pl.BlockSpec(memory_space=pltpu.SMEM)],
        out_specs=(spec, spec),
        scratch_shapes=[
            vm((hid, 2 * width), bf16),
            vm((hid, width), bf16),
            vm((peers, 1, slots), jnp.int32),
            vm((edges,), jnp.int32),
            vm((edges,), jnp.int32),
            vm((1, halos), jnp.int32),
            dma((7,)),
            vm((rows, width), bf16),
            vm((rows, width), bf16),
            vm((rows, edges), bf16),
            vm((halos, edges), bf16),
            vm((rows, edges), bf16),
            vm((rows, halos), bf16),
            vm((2 * hid, edges), bf16),
            vm((hid, edges), f32),
            vm((hid, edges), f32),
            vm((halos, hid), f32),
            vm((halos, hid), f32),
            vm((halos, hid), bf16),
            vm((halos, hid), bf16),
            vm((hid, 3 * width), bf16),
            vm((parts, chunk, 3 * width), bf16),
            vm((chunk, 3 * width), bf16),
            vm((hid, 3 * width), bf16),
            vm((rows, width), f32),
            vm((rows, width), bf16),
            vm((tps, rows, feat), bf16),
            dma((tps,)), dma((tps,)), dma((tps,)), dma((tps,)),
            dma((peers,)), dma((peers,)), dma((peers,)), dma((peers,)),
            dma((2, parts)), dma((2, parts)), dma((2, parts)), dma((2, parts)),
            dma((tps,)), dma((tps,)),
        ],
        compiler_params=pltpu.CompilerParams(
            collective_id=0, has_side_effects=True, vmem_limit_bytes=48 * 1024 * 1024
        ),
    )(
        *operands, edge_count
    )
    return pl.pallas_call(
        functools.partial(write_kernel, scale),
        out_shape=(
            jax.ShapeDtypeStruct((rows, feat), bf16),
            jax.ShapeDtypeStruct((hid, 2 * width), f32),
            jax.ShapeDtypeStruct((hid, width), f32),
        ),
        in_specs=[spec, spec],
        out_specs=(hbm, hbm, hbm),
        scratch_shapes=[vm((hid, 2 * width), f32), vm((hid, width), f32), dma((3,))],
        compiler_params=pltpu.CompilerParams(vmem_limit_bytes=4 * 1024 * 1024),
    )(node, total)


def layer(node_state, cotangent, w_in, w_out, send_list, sender, receiver, edge_count):
    parts = lax.axis_size("dom")
    fits = (
        node_state.shape[1] % 128 == 0
        and node_state.shape[0] % 16 == 0
        and send_list.shape[2] % 16 == 0
        and w_in.shape[0] % (16 * parts) == 0
        and sender.shape[0] % 128 == 0
    )
    plan = fused if fits else per_device
    return plan(node_state, cotangent, w_in, w_out, send_list, sender, receiver, edge_count)


def solution(mesh):
    return jax.shard_map(
        layer,
        mesh=mesh,
        in_specs=(
            P("dom", "tensor"),
            P("dom", "tensor"),
            P("tensor", None),
            P("tensor", None),
            P("dom", None, None),
            P("dom"),
            P("dom"),
            P("dom"),
        ),
        out_specs=(P("dom", "tensor"), P("tensor", None), P("tensor", None)),
        check_vma=False,
    )
```

```python
import functools

import jax
import jax.numpy as jnp
from jax import lax
from jax.experimental import pallas as pl
from jax.experimental.pallas import tpu as pltpu
from jax.sharding import PartitionSpec as P


def shifted(value, axis, steps):
    count = lax.axis_size(axis)
    pairs = [(source, (source + steps) % count) for source in range(count)]
    return lax.ppermute(value, axis, pairs)


def contract_rows(left, right):
    return lax.dot_general(
        left, right, (((0,), (0,)), ((), ())), preferred_element_type=jnp.float32
    )


def contract_cols(left, right):
    return lax.dot_general(
        left, right, (((1,), (1,)), ((), ())), preferred_element_type=jnp.float32
    )


def neighbour_offsets(count):
    return [1, count - 1, 2, count - 2, 3, count - 3, count // 2]


def per_device(node_state, cotangent, w_in, w_out, send_list, sender, receiver, edge_count):
    local_rows = node_state.shape[0]
    slots = send_list.shape[2]
    peers = send_list.shape[1]
    parts = lax.axis_size("dom")
    offsets = neighbour_offsets(parts)
    my_list = send_list[0]
    arrived = []
    for which, offset in enumerate(offsets):
        arrived.append(shifted(node_state[my_list[which]], "dom", offset))
    incoming = jnp.concatenate(arrived, 0)
    table_part = jnp.concatenate([node_state, incoming], 0)
    table, cot_full = (
        lax.all_gather(table_part, "tensor", axis=1, tiled=True),
        lax.all_gather(cotangent, "tensor", axis=1, tiled=True),
    )
    width = table.shape[1]
    rows = table.shape[0]
    w_send = w_in[:, :width]
    w_recv = w_in[:, width:]
    sent = table[sender]
    recv = table[receiver]
    pre = contract_cols(sent, w_send) + contract_cols(recv, w_recv)
    sig = jax.nn.sigmoid(pre)
    act = (pre * sig).astype(jnp.bfloat16)
    slope = sig * (1.0 + pre * (1.0 - sig))
    live = (jnp.arange(sender.shape[0], dtype=jnp.int32) < edge_count[0]).astype(jnp.bfloat16)
    message_grad = cot_full[receiver] * live[:, None]
    out_grad = contract_rows(act, message_grad)
    hidden_grad = contract_cols(message_grad, w_out)
    pre_grad = (hidden_grad * slope).astype(jnp.bfloat16)
    in_grad = jnp.concatenate([contract_rows(pre_grad, sent), contract_rows(pre_grad, recv)], 1)
    hit_send = (sender[:, None] == jnp.arange(rows, dtype=jnp.int32)[None, :]).astype(jnp.bfloat16)
    hit_recv = (receiver[:, None] == jnp.arange(local_rows, dtype=jnp.int32)[None, :]).astype(
        jnp.bfloat16
    )
    send_sum = contract_rows(hit_send, pre_grad).astype(jnp.bfloat16)
    recv_sum = contract_rows(hit_recv, pre_grad).astype(jnp.bfloat16)
    term = jnp.dot(send_sum, w_send, preferred_element_type=jnp.float32)
    term = term.at[:local_rows].add(jnp.dot(recv_sum, w_recv, preferred_element_type=jnp.float32))
    row_grad = lax.psum_scatter(term, "tensor", scatter_dimension=1, tiled=True)
    feat_part = row_grad.shape[1]
    halo_grad = row_grad[local_rows:].reshape(peers, slots, feat_part)
    node_grad = cotangent.astype(jnp.float32) + row_grad[:local_rows]
    for which, offset in enumerate(offsets):
        returned = shifted(halo_grad[which], "dom", parts - offset)
        node_grad = node_grad.at[my_list[which]].add(returned)
    sum_in, sum_out = lax.psum((in_grad, out_grad), "dom")
    scale = float(sender.shape[0] * parts) ** (-0.5)
    return (node_grad.astype(jnp.bfloat16), sum_in * scale, sum_out * scale)


MESH = pl.DeviceIdType.MESH


def dot(left, right):
    return jnp.dot(left, right, preferred_element_type=jnp.float32)


def split(value):
    high = value.astype(jnp.bfloat16)
    low = (value - high.astype(jnp.float32)).astype(jnp.bfloat16)
    return jnp.concatenate([high, low], 0)


def layer_kernel(
    parts, tps, offsets, slots,
    x_ref, c_ref, win_any, wout_any, list_any, send_any, recv_any, count_ref,
    node_ref, ag_ref,
    win_ref, wout_ref, list_ref, send_ref, recv_ref, spot_ref, load_s, xf, cf, st_loc, st_hal, rt, lt, ap, pre_buf, hid_buf,
    halo_out, halo_in, back_out, back_in, sums, rs, ag_out, ag, part_f, part_b, part_in,
    gx_s, gx_r, gc_s, gc_r, h_s, h_r, b_s, b_r, rs_s, rs_r, ag_s, ag_r, p_s, p_r, mid_out, mid_in, m_s, m_r,
):
    me = lax.axis_index("dom")
    mt = lax.axis_index("tensor")
    rows, feat = x_ref.shape
    hid = win_ref.shape[0]
    width = feat * tps
    edges = send_ref.shape[0]
    peers = len(offsets)
    halos = peers * slots
    squad = parts // 2
    seat = lax.rem(me, squad)
    base = me - seat
    chunk = hid // squad
    tile = 512 if edges % 512 == 0 else edges
    tiles = [slice(i, i + tile) for i in range(0, edges, tile)]

    def mod(value, count):
        return lax.rem(value + count, count)

    def copy(src, dst, ss, rsem, **where):
        return pltpu.make_async_remote_copy(
            src_ref=src, dst_ref=dst, send_sem=ss, recv_sem=rsem,
            device_id=where, device_id_type=MESH,
        )

    barrier = pltpu.get_barrier_semaphore()
    for k in range(1, tps):
        pl.semaphore_signal(barrier, inc=1, device_id={"tensor": mod(mt + k, tps)}, device_id_type=MESH)
    for k in range(1, parts):
        pl.semaphore_signal(barrier, inc=1, device_id={"dom": mod(me + k, parts)}, device_id_type=MESH)

    mine = pl.ds(pl.multiple_of(mt * feat, feat), feat)
    pairs = [
        (list_any, list_ref), (send_any, send_ref), (recv_any, recv_ref),
        (x_ref, xf.at[:, mine]), (win_any, win_ref), (c_ref, cf.at[:, mine]), (wout_any, wout_ref),
    ]
    loads = [pltpu.make_async_copy(a, b, load_s.at[i]) for i, (a, b) in enumerate(pairs)]
    for item in loads:
        item.start()
    pl.semaphore_wait(barrier, tps - 1 + parts - 1)

    x_copies = [
        copy(x_ref, xf.at[:, mine], gx_s.at[k], gx_r.at[k], tensor=mod(mt + k, tps))
        for k in range(1, tps)
    ]
    c_copies = [
        copy(c_ref, cf.at[:, mine], gc_s.at[k], gc_r.at[k], tensor=mod(mt + k, tps))
        for k in range(1, tps)
    ]
    for item in x_copies + c_copies:
        item.start()

    def hits(index, first, count):
        lanes = index.shape[1]
        spot = lax.broadcasted_iota(jnp.int32, (count, lanes), 0) + first
        return jnp.where(spot == index, 1.0, 0.0).astype(jnp.bfloat16)

    for item in loads[:3]:
        item.wait()
    for j in range(peers):
        spot_ref[:, j * slots:(j + 1) * slots] = list_ref[j]
    lt[...] = hits(spot_ref[...], 0, rows)
    count = count_ref[0]
    for cols in tiles:
        where = lax.broadcasted_iota(jnp.int32, (1, tile), 1) + cols.start
        target = jnp.where(where < count, recv_ref[cols].reshape(1, tile), -1)
        rt[:, cols] = hits(target, 0, rows)
        sends = send_ref[cols].reshape(1, tile)
        st_loc[:, cols] = hits(sends, 0, rows)
        st_hal[:, cols] = hits(sends, rows, halos)

    for item in loads[3:5]:
        item.wait()
    for item in x_copies:
        item.wait_recv()
    own = split(contract_cols(win_ref[:, :width], xf[...]))
    picked = dot(own, lt[...])
    halo_out[...] = (picked[:hid] + picked[hid:]).T
    h_copies = []
    for j, offset in enumerate(offsets):
        band = slice(j * slots, (j + 1) * slots)
        item = copy(
            halo_out.at[band], halo_in.at[band], h_s.at[j], h_r.at[j],
            dom=mod(me + offset, parts),
        )
        item.start()
        h_copies.append(item)

    at_recv = split(contract_cols(win_ref[:, width:], xf[...]))
    for cols in tiles:
        both = dot(own, st_loc[:, cols]) + dot(at_recv, rt[:, cols])
        pre_buf[:, cols] = both[:hid] + both[hid:]
    for item in loads[5:]:
        item.wait()
    for item in c_copies:
        item.wait_recv()
    grad = split(contract_cols(wout_ref[...], cf[...]))
    for cols in tiles:
        both = dot(grad, rt[:, cols])
        hid_buf[:, cols] = both[:hid] + both[hid:]

    for item in h_copies:
        item.wait_recv()
    far = split(halo_in[...].T)
    for cols in tiles:
        both = dot(far, st_hal[:, cols])
        pre = pre_buf[:, cols] + both[:hid] + both[hid:]
        sig = jax.nn.sigmoid(pre)
        slope = sig * (1.0 + pre * (1.0 - sig))
        ap[:hid, cols] = (pre * sig).astype(jnp.bfloat16)
        ap[hid:, cols] = (hid_buf[:, cols] * slope).astype(jnp.bfloat16)

    back_out[...] = contract_cols(st_hal[...], ap[hid:]).astype(jnp.bfloat16)
    b_copies = []
    for j, offset in enumerate(offsets):
        band = slice(j * slots, (j + 1) * slots)
        item = copy(
            back_out.at[band], back_in.at[band], b_s.at[j], b_r.at[j],
            dom=mod(me - offset, parts),
        )
        item.start()
        b_copies.append(item)

    spans = [slice(width, 3 * width), slice(0, width)]

    def scatter(which):
        out = []
        for k in range(1, squad):
            peer = mod(seat + k, squad)
            band = pl.ds(pl.multiple_of(peer * chunk, chunk), chunk)
            item = copy(
                sums.at[band, spans[which]], rs.at[k, :, spans[which]],
                rs_s.at[which, k], rs_r.at[which, k], dom=base + peer,
            )
            item.start()
            out.append(item)
        return out

    ours = pl.ds(pl.multiple_of(seat * chunk, chunk), chunk)

    def swap(which, arrivals):
        span = spans[which]
        total = sums[ours, span].astype(jnp.float32)
        for k, item in enumerate(arrivals):
            item.wait_recv()
            total = total + rs[k + 1, :, span].astype(jnp.float32)
        mid_out[:, span] = total.astype(jnp.bfloat16)
        item = copy(
            mid_out.at[:, span], mid_in.at[:, span], m_s.at[which], m_r.at[which],
            dom=mod(me + squad, parts),
        )
        item.start()
        return item

    def spread(which, arrival):
        span = spans[which]
        arrival.wait_recv()
        total = mid_out[:, span].astype(jnp.float32) + mid_in[:, span].astype(jnp.float32)
        total = total.astype(jnp.bfloat16)
        ag_out[:, span] = total
        ag[ours, span] = total
        out = []
        for k in range(1, squad):
            item = copy(
                ag_out.at[:, span], ag.at[ours, span],
                ag_s.at[which, k], ag_r.at[which, k], dom=base + mod(seat + k, squad),
            )
            item.start()
            out.append(item)
        return out

    at_node = contract_cols(ap[...], rt[...])
    act_sum = at_node[:hid].astype(jnp.bfloat16)
    recv_sum = at_node[hid:].astype(jnp.bfloat16)
    sums[:, 2 * width:] = dot(act_sum, cf[...]).astype(jnp.bfloat16)
    sums[:, width:2 * width] = dot(recv_sum, xf[...]).astype(jnp.bfloat16)
    first = scatter(0)
    near = contract_cols(ap[hid:], st_loc[...])
    part_f[...] = dot(at_node[hid:].T.astype(jnp.bfloat16), win_ref[:, width:])

    for item in b_copies:
        item.wait_recv()
    returned = back_in[...].astype(jnp.float32).T.astype(jnp.bfloat16)
    whole = near + contract_cols(returned, lt[...])
    sums[:, :width] = dot(whole.astype(jnp.bfloat16), xf[...]).astype(jnp.bfloat16)
    second = scatter(1)
    share = part_f[...] + dot(whole.T.astype(jnp.bfloat16), win_ref[:, :width])
    part_f[...] = share
    part_b[...] = share.astype(jnp.bfloat16)
    p_copies = []
    for k in range(1, tps):
        peer = mod(mt + k, tps)
        theirs = pl.ds(pl.multiple_of(peer * feat, feat), feat)
        item = copy(part_b.at[:, theirs], part_in.at[k], p_s.at[k], p_r.at[k], tensor=peer)
        item.start()
        p_copies.append(item)

    swaps = [swap(0, first), swap(1, second)]
    gathers = spread(0, swaps[0])
    node = cf[:, mine].astype(jnp.float32) + part_f[:, mine]
    for k, item in enumerate(p_copies):
        item.wait_recv()
        node = node + part_in[k + 1].astype(jnp.float32)
    node_ref[...] = node.astype(jnp.bfloat16)
    gathers += spread(1, swaps[1])
    for item in gathers:
        item.wait_recv()
    ag_ref[...] = ag[...]
    for item in x_copies + c_copies + h_copies + b_copies + first + second + p_copies + swaps + gathers:
        item.wait_send()


def write_kernel(scale, node_ref, ag_ref, node_any, gin_any, gout_any, gin_ref, gout_ref, sems):
    cut = gin_ref.shape[1]
    node_copy = pltpu.make_async_copy(node_ref, node_any, sems.at[0])
    node_copy.start()
    gin_ref[...] = ag_ref[:, :cut].astype(jnp.float32) * scale
    gin_copy = pltpu.make_async_copy(gin_ref, gin_any, sems.at[1])
    gin_copy.start()
    gout_ref[...] = ag_ref[:, cut:].astype(jnp.float32) * scale
    gout_copy = pltpu.make_async_copy(gout_ref, gout_any, sems.at[2])
    gout_copy.start()
    node_copy.wait()
    gin_copy.wait()
    gout_copy.wait()


def fused(node_state, cotangent, w_in, w_out, send_list, sender, receiver, edge_count):
    parts = lax.axis_size("dom")
    tps = lax.axis_size("tensor")
    rows, feat = node_state.shape
    hid = w_in.shape[0]
    width = feat * tps
    edges = sender.shape[0]
    _, peers, slots = send_list.shape
    halos = peers * slots
    offsets = neighbour_offsets(parts)
    squad = parts // 2
    chunk = hid // squad
    scale = float(edges * parts) ** (-0.5)
    bf16, f32 = jnp.bfloat16, jnp.float32
    vm, dma = pltpu.VMEM, pltpu.SemaphoreType.DMA
    spec = pl.BlockSpec(memory_space=pltpu.VMEM)
    hbm = pl.BlockSpec(memory_space=pltpu.HBM)
    operands = [
        pltpu.with_memory_space_constraint(item, pltpu.HBM)
        for item in (
            node_state, cotangent, w_in, w_out, send_list.transpose(1, 0, 2),
            sender, receiver,
        )
    ]
    node, total = pl.pallas_call(
        functools.partial(layer_kernel, parts, tps, offsets, slots),
        out_shape=(
            jax.ShapeDtypeStruct((rows, feat), bf16),
            jax.ShapeDtypeStruct((hid, 3 * width), bf16),
        ),
        in_specs=[hbm] * 7 + [pl.BlockSpec(memory_space=pltpu.SMEM)],
        out_specs=(spec, spec),
        scratch_shapes=[
            vm((hid, 2 * width), bf16),
            vm((hid, width), bf16),
            vm((peers, 1, slots), jnp.int32),
            vm((edges,), jnp.int32),
            vm((edges,), jnp.int32),
            vm((1, halos), jnp.int32),
            dma((7,)),
            vm((rows, width), bf16),
            vm((rows, width), bf16),
            vm((rows, edges), bf16),
            vm((halos, edges), bf16),
            vm((rows, edges), bf16),
            vm((rows, halos), bf16),
            vm((2 * hid, edges), bf16),
            vm((hid, edges), f32),
            vm((hid, edges), f32),
            vm((halos, hid), f32),
            vm((halos, hid), f32),
            vm((halos, hid), bf16),
            vm((halos, hid), bf16),
            vm((hid, 3 * width), bf16),
            vm((squad, chunk, 3 * width), bf16),
            vm((chunk, 3 * width), bf16),
            vm((hid, 3 * width), bf16),
            vm((rows, width), f32),
            vm((rows, width), bf16),
            vm((tps, rows, feat), bf16),
            dma((tps,)), dma((tps,)), dma((tps,)), dma((tps,)),
            dma((peers,)), dma((peers,)), dma((peers,)), dma((peers,)),
            dma((2, squad)), dma((2, squad)), dma((2, squad)), dma((2, squad)),
            dma((tps,)), dma((tps,)),
            vm((chunk, 3 * width), bf16), vm((chunk, 3 * width), bf16), dma((2,)), dma((2,)),
        ],
        compiler_params=pltpu.CompilerParams(
            collective_id=0, has_side_effects=True, vmem_limit_bytes=48 * 1024 * 1024
        ),
    )(
        *operands, edge_count
    )
    return pl.pallas_call(
        functools.partial(write_kernel, scale),
        out_shape=(
            jax.ShapeDtypeStruct((rows, feat), bf16),
            jax.ShapeDtypeStruct((hid, 2 * width), f32),
            jax.ShapeDtypeStruct((hid, width), f32),
        ),
        in_specs=[spec, spec],
        out_specs=(hbm, hbm, hbm),
        scratch_shapes=[vm((hid, 2 * width), f32), vm((hid, width), f32), dma((3,))],
        compiler_params=pltpu.CompilerParams(vmem_limit_bytes=4 * 1024 * 1024),
    )(node, total)


def layer(node_state, cotangent, w_in, w_out, send_list, sender, receiver, edge_count):
    parts = lax.axis_size("dom")
    fits = (
        node_state.shape[1] % 128 == 0
        and node_state.shape[0] % 16 == 0
        and send_list.shape[2] % 16 == 0
        and parts % 2 == 0
        and w_in.shape[0] % (16 * parts) == 0
        and sender.shape[0] % 128 == 0
    )
    plan = fused if fits else per_device
    return plan(node_state, cotangent, w_in, w_out, send_list, sender, receiver, edge_count)


def solution(mesh):
    return jax.shard_map(
        layer,
        mesh=mesh,
        in_specs=(
            P("dom", "tensor"),
            P("dom", "tensor"),
            P("tensor", None),
            P("tensor", None),
            P("dom", None, None),
            P("dom"),
            P("dom"),
            P("dom"),
        ),
        out_specs=(P("dom", "tensor"), P("tensor", None), P("tensor", None)),
        check_vma=False,
    )
```

```python
import functools

import jax
import jax.numpy as jnp
from jax import lax
from jax.experimental import pallas as pl
from jax.experimental.pallas import tpu as pltpu
from jax.sharding import PartitionSpec as P


def shifted(value, axis, steps):
    count = lax.axis_size(axis)
    pairs = [(source, (source + steps) % count) for source in range(count)]
    return lax.ppermute(value, axis, pairs)


def contract_rows(left, right):
    return lax.dot_general(
        left, right, (((0,), (0,)), ((), ())), preferred_element_type=jnp.float32
    )


def contract_cols(left, right):
    return lax.dot_general(
        left, right, (((1,), (1,)), ((), ())), preferred_element_type=jnp.float32
    )


def neighbour_offsets(count):
    return [1, count - 1, 2, count - 2, 3, count - 3, count // 2]


def per_device(node_state, cotangent, w_in, w_out, send_list, sender, receiver, edge_count):
    local_rows = node_state.shape[0]
    slots = send_list.shape[2]
    peers = send_list.shape[1]
    parts = lax.axis_size("dom")
    offsets = neighbour_offsets(parts)
    my_list = send_list[0]
    arrived = []
    for which, offset in enumerate(offsets):
        arrived.append(shifted(node_state[my_list[which]], "dom", offset))
    incoming = jnp.concatenate(arrived, 0)
    table_part = jnp.concatenate([node_state, incoming], 0)
    table, cot_full = (
        lax.all_gather(table_part, "tensor", axis=1, tiled=True),
        lax.all_gather(cotangent, "tensor", axis=1, tiled=True),
    )
    width = table.shape[1]
    rows = table.shape[0]
    w_send = w_in[:, :width]
    w_recv = w_in[:, width:]
    sent = table[sender]
    recv = table[receiver]
    pre = contract_cols(sent, w_send) + contract_cols(recv, w_recv)
    sig = jax.nn.sigmoid(pre)
    act = (pre * sig).astype(jnp.bfloat16)
    slope = sig * (1.0 + pre * (1.0 - sig))
    live = (jnp.arange(sender.shape[0], dtype=jnp.int32) < edge_count[0]).astype(jnp.bfloat16)
    message_grad = cot_full[receiver] * live[:, None]
    out_grad = contract_rows(act, message_grad)
    hidden_grad = contract_cols(message_grad, w_out)
    pre_grad = (hidden_grad * slope).astype(jnp.bfloat16)
    in_grad = jnp.concatenate([contract_rows(pre_grad, sent), contract_rows(pre_grad, recv)], 1)
    hit_send = (sender[:, None] == jnp.arange(rows, dtype=jnp.int32)[None, :]).astype(jnp.bfloat16)
    hit_recv = (receiver[:, None] == jnp.arange(local_rows, dtype=jnp.int32)[None, :]).astype(
        jnp.bfloat16
    )
    send_sum = contract_rows(hit_send, pre_grad).astype(jnp.bfloat16)
    recv_sum = contract_rows(hit_recv, pre_grad).astype(jnp.bfloat16)
    term = jnp.dot(send_sum, w_send, preferred_element_type=jnp.float32)
    term = term.at[:local_rows].add(jnp.dot(recv_sum, w_recv, preferred_element_type=jnp.float32))
    row_grad = lax.psum_scatter(term, "tensor", scatter_dimension=1, tiled=True)
    feat_part = row_grad.shape[1]
    halo_grad = row_grad[local_rows:].reshape(peers, slots, feat_part)
    node_grad = cotangent.astype(jnp.float32) + row_grad[:local_rows]
    for which, offset in enumerate(offsets):
        returned = shifted(halo_grad[which], "dom", parts - offset)
        node_grad = node_grad.at[my_list[which]].add(returned)
    sum_in, sum_out = lax.psum((in_grad, out_grad), "dom")
    scale = float(sender.shape[0] * parts) ** (-0.5)
    return (node_grad.astype(jnp.bfloat16), sum_in * scale, sum_out * scale)


MESH = pl.DeviceIdType.MESH


def dot(left, right):
    return jnp.dot(left, right, preferred_element_type=jnp.float32)


def split(value):
    high = value.astype(jnp.bfloat16)
    low = (value - high.astype(jnp.float32)).astype(jnp.bfloat16)
    return jnp.concatenate([high, low], 0)


def layer_kernel(
    parts, tps, offsets, slots,
    x_ref, c_ref, win_any, wout_any, list_any, send_any, recv_any, count_ref,
    node_ref, ag_ref,
    win_ref, wout_ref, list_ref, send_ref, recv_ref, spot_ref, load_s, xf, cf, st_loc, st_hal, rt, lt, ap, pre_buf, hid_buf,
    halo_out, halo_in, back_out, back_in, sums, rs, ag_out, ag, part_f, part_b, part_in,
    gx_s, gx_r, gc_s, gc_r, h_s, h_r, b_s, b_r, rs_s, rs_r, ag_s, ag_r, p_s, p_r, mid_out, mid_in, m_s, m_r,
):
    me = lax.axis_index("dom")
    mt = lax.axis_index("tensor")
    rows, feat = x_ref.shape
    hid = win_ref.shape[0]
    width = feat * tps
    edges = send_ref.shape[0]
    peers = len(offsets)
    halos = peers * slots
    squad = parts // 2
    seat = lax.rem(me, squad)
    base = me - seat
    chunk = hid // squad
    tile = 512 if edges % 512 == 0 else edges
    tiles = [slice(i, i + tile) for i in range(0, edges, tile)]

    def mod(value, count):
        return lax.rem(value + count, count)

    def copy(src, dst, ss, rsem, **where):
        return pltpu.make_async_remote_copy(
            src_ref=src, dst_ref=dst, send_sem=ss, recv_sem=rsem,
            device_id=where, device_id_type=MESH,
        )

    barrier = pltpu.get_barrier_semaphore()
    for k in range(1, tps):
        pl.semaphore_signal(barrier, inc=1, device_id={"tensor": mod(mt + k, tps)}, device_id_type=MESH)
    for k in range(1, parts):
        pl.semaphore_signal(barrier, inc=1, device_id={"dom": mod(me + k, parts)}, device_id_type=MESH)

    mine = pl.ds(pl.multiple_of(mt * feat, feat), feat)
    pairs = [
        (list_any, list_ref), (send_any, send_ref), (recv_any, recv_ref),
        (x_ref, xf.at[:, mine]), (win_any, win_ref), (c_ref, cf.at[:, mine]), (wout_any, wout_ref),
    ]
    loads = [pltpu.make_async_copy(a, b, load_s.at[i]) for i, (a, b) in enumerate(pairs)]
    for item in loads:
        item.start()
    pl.semaphore_wait(barrier, tps - 1 + parts - 1)

    x_copies = [
        copy(x_ref, xf.at[:, mine], gx_s.at[k], gx_r.at[k], tensor=mod(mt + k, tps))
        for k in range(1, tps)
    ]
    c_copies = [
        copy(c_ref, cf.at[:, mine], gc_s.at[k], gc_r.at[k], tensor=mod(mt + k, tps))
        for k in range(1, tps)
    ]
    for item in x_copies + c_copies:
        item.start()

    def hits(index, first, count):
        lanes = index.shape[1]
        spot = lax.broadcasted_iota(jnp.int32, (count, lanes), 0) + first
        return jnp.where(spot == index, 1.0, 0.0).astype(jnp.bfloat16)

    for item in loads[:3]:
        item.wait()
    for j in range(peers):
        spot_ref[:, j * slots:(j + 1) * slots] = list_ref[j]
    lt[...] = hits(spot_ref[...], 0, rows)
    count = count_ref[0]
    for cols in tiles:
        where = lax.broadcasted_iota(jnp.int32, (1, tile), 1) + cols.start
        target = jnp.where(where < count, recv_ref[cols].reshape(1, tile), -1)
        rt[:, cols] = hits(target, 0, rows)
        sends = send_ref[cols].reshape(1, tile)
        st_loc[:, cols] = hits(sends, 0, rows)
        st_hal[:, cols] = hits(sends, rows, halos)

    for item in loads[3:5]:
        item.wait()
    for item in x_copies:
        item.wait_recv()
    own = split(contract_cols(win_ref[:, :width], xf[...]))
    picked = dot(own, lt[...])
    halo_out[...] = (picked[:hid] + picked[hid:]).T
    h_copies = []
    for j, offset in enumerate(offsets):
        band = slice(j * slots, (j + 1) * slots)
        item = copy(
            halo_out.at[band], halo_in.at[band], h_s.at[j], h_r.at[j],
            dom=mod(me + offset, parts),
        )
        item.start()
        h_copies.append(item)

    at_recv = split(contract_cols(win_ref[:, width:], xf[...]))
    for cols in tiles:
        both = dot(own, st_loc[:, cols]) + dot(at_recv, rt[:, cols])
        pre_buf[:, cols] = both[:hid] + both[hid:]
    for item in loads[5:]:
        item.wait()
    for item in c_copies:
        item.wait_recv()
    grad = split(contract_cols(wout_ref[...], cf[...]))
    for cols in tiles:
        both = dot(grad, rt[:, cols])
        hid_buf[:, cols] = both[:hid] + both[hid:]

    for item in h_copies:
        item.wait_recv()
    far = split(halo_in[...].T)
    for cols in tiles:
        both = dot(far, st_hal[:, cols])
        pre = pre_buf[:, cols] + both[:hid] + both[hid:]
        sig = jax.nn.sigmoid(pre)
        slope = sig * (1.0 + pre * (1.0 - sig))
        ap[:hid, cols] = (pre * sig).astype(jnp.bfloat16)
        ap[hid:, cols] = (hid_buf[:, cols] * slope).astype(jnp.bfloat16)

    back_out[...] = contract_cols(st_hal[...], ap[hid:]).astype(jnp.bfloat16)
    b_copies = []
    for j, offset in enumerate(offsets):
        band = slice(j * slots, (j + 1) * slots)
        item = copy(
            back_out.at[band], back_in.at[band], b_s.at[j], b_r.at[j],
            dom=mod(me - offset, parts),
        )
        item.start()
        b_copies.append(item)

    spans = [slice(2 * width, 3 * width), slice(width, 2 * width), slice(0, width)]

    def scatter(which):
        out = []
        for k in range(1, squad):
            peer = mod(seat + k, squad)
            band = pl.ds(pl.multiple_of(peer * chunk, chunk), chunk)
            item = copy(
                sums.at[band, spans[which]], rs.at[k, :, spans[which]],
                rs_s.at[which, k], rs_r.at[which, k], dom=base + peer,
            )
            item.start()
            out.append(item)
        return out

    ours = pl.ds(pl.multiple_of(seat * chunk, chunk), chunk)

    def swap(which, arrivals):
        span = spans[which]
        total = sums[ours, span].astype(jnp.float32)
        for k, item in enumerate(arrivals):
            item.wait_recv()
            total = total + rs[k + 1, :, span].astype(jnp.float32)
        mid_out[:, span] = total.astype(jnp.bfloat16)
        item = copy(
            mid_out.at[:, span], mid_in.at[:, span], m_s.at[which], m_r.at[which],
            dom=mod(me + squad, parts),
        )
        item.start()
        return item

    def spread(which, arrival):
        span = spans[which]
        arrival.wait_recv()
        total = mid_out[:, span].astype(jnp.float32) + mid_in[:, span].astype(jnp.float32)
        total = total.astype(jnp.bfloat16)
        ag_out[:, span] = total
        ag[ours, span] = total
        out = []
        for k in range(1, squad):
            item = copy(
                ag_out.at[:, span], ag.at[ours, span],
                ag_s.at[which, k], ag_r.at[which, k], dom=base + mod(seat + k, squad),
            )
            item.start()
            out.append(item)
        return out

    at_node = contract_cols(ap[...], rt[...])
    act_sum = at_node[:hid].astype(jnp.bfloat16)
    recv_sum = at_node[hid:].astype(jnp.bfloat16)
    sums[:, 2 * width:] = dot(act_sum, cf[...]).astype(jnp.bfloat16)
    first = scatter(0)
    sums[:, width:2 * width] = dot(recv_sum, xf[...]).astype(jnp.bfloat16)
    second = scatter(1)
    near = contract_cols(ap[hid:], st_loc[...])
    part_f[...] = dot(at_node[hid:].T.astype(jnp.bfloat16), win_ref[:, width:])

    for item in b_copies:
        item.wait_recv()
    returned = back_in[...].astype(jnp.float32).T.astype(jnp.bfloat16)
    whole = near + contract_cols(returned, lt[...])
    sums[:, :width] = dot(whole.astype(jnp.bfloat16), xf[...]).astype(jnp.bfloat16)
    third = scatter(2)
    share = part_f[...] + dot(whole.T.astype(jnp.bfloat16), win_ref[:, :width])
    part_f[...] = share
    part_b[...] = share.astype(jnp.bfloat16)
    p_copies = []
    for k in range(1, tps):
        peer = mod(mt + k, tps)
        theirs = pl.ds(pl.multiple_of(peer * feat, feat), feat)
        item = copy(part_b.at[:, theirs], part_in.at[k], p_s.at[k], p_r.at[k], tensor=peer)
        item.start()
        p_copies.append(item)

    swaps = [swap(0, first), swap(1, second)]
    gathers = spread(0, swaps[0])
    swaps.append(swap(2, third))
    gathers += spread(1, swaps[1])
    node = cf[:, mine].astype(jnp.float32) + part_f[:, mine]
    for k, item in enumerate(p_copies):
        item.wait_recv()
        node = node + part_in[k + 1].astype(jnp.float32)
    node_ref[...] = node.astype(jnp.bfloat16)
    gathers += spread(2, swaps[2])
    for item in gathers:
        item.wait_recv()
    ag_ref[...] = ag[...]
    for item in x_copies + c_copies + h_copies + b_copies + first + second + third + p_copies + swaps + gathers:
        item.wait_send()


def write_kernel(scale, node_ref, ag_ref, node_any, gin_any, gout_any, gin_ref, gout_ref, sems):
    cut = gin_ref.shape[1]
    node_copy = pltpu.make_async_copy(node_ref, node_any, sems.at[0])
    node_copy.start()
    gin_ref[...] = ag_ref[:, :cut].astype(jnp.float32) * scale
    gin_copy = pltpu.make_async_copy(gin_ref, gin_any, sems.at[1])
    gin_copy.start()
    gout_ref[...] = ag_ref[:, cut:].astype(jnp.float32) * scale
    gout_copy = pltpu.make_async_copy(gout_ref, gout_any, sems.at[2])
    gout_copy.start()
    node_copy.wait()
    gin_copy.wait()
    gout_copy.wait()


def fused(node_state, cotangent, w_in, w_out, send_list, sender, receiver, edge_count):
    parts = lax.axis_size("dom")
    tps = lax.axis_size("tensor")
    rows, feat = node_state.shape
    hid = w_in.shape[0]
    width = feat * tps
    edges = sender.shape[0]
    _, peers, slots = send_list.shape
    halos = peers * slots
    offsets = neighbour_offsets(parts)
    squad = parts // 2
    chunk = hid // squad
    scale = float(edges * parts) ** (-0.5)
    bf16, f32 = jnp.bfloat16, jnp.float32
    vm, dma = pltpu.VMEM, pltpu.SemaphoreType.DMA
    spec = pl.BlockSpec(memory_space=pltpu.VMEM)
    hbm = pl.BlockSpec(memory_space=pltpu.HBM)
    operands = [
        pltpu.with_memory_space_constraint(item, pltpu.HBM)
        for item in (
            node_state, cotangent, w_in, w_out, send_list.transpose(1, 0, 2),
            sender, receiver,
        )
    ]
    node, total = pl.pallas_call(
        functools.partial(layer_kernel, parts, tps, offsets, slots),
        out_shape=(
            jax.ShapeDtypeStruct((rows, feat), bf16),
            jax.ShapeDtypeStruct((hid, 3 * width), bf16),
        ),
        in_specs=[hbm] * 7 + [pl.BlockSpec(memory_space=pltpu.SMEM)],
        out_specs=(spec, spec),
        scratch_shapes=[
            vm((hid, 2 * width), bf16),
            vm((hid, width), bf16),
            vm((peers, 1, slots), jnp.int32),
            vm((edges,), jnp.int32),
            vm((edges,), jnp.int32),
            vm((1, halos), jnp.int32),
            dma((7,)),
            vm((rows, width), bf16),
            vm((rows, width), bf16),
            vm((rows, edges), bf16),
            vm((halos, edges), bf16),
            vm((rows, edges), bf16),
            vm((rows, halos), bf16),
            vm((2 * hid, edges), bf16),
            vm((hid, edges), f32),
            vm((hid, edges), f32),
            vm((halos, hid), f32),
            vm((halos, hid), f32),
            vm((halos, hid), bf16),
            vm((halos, hid), bf16),
            vm((hid, 3 * width), bf16),
            vm((squad, chunk, 3 * width), bf16),
            vm((chunk, 3 * width), bf16),
            vm((hid, 3 * width), bf16),
            vm((rows, width), f32),
            vm((rows, width), bf16),
            vm((tps, rows, feat), bf16),
            dma((tps,)), dma((tps,)), dma((tps,)), dma((tps,)),
            dma((peers,)), dma((peers,)), dma((peers,)), dma((peers,)),
            dma((3, squad)), dma((3, squad)), dma((3, squad)), dma((3, squad)),
            dma((tps,)), dma((tps,)),
            vm((chunk, 3 * width), bf16), vm((chunk, 3 * width), bf16), dma((3,)), dma((3,)),
        ],
        compiler_params=pltpu.CompilerParams(
            collective_id=0, has_side_effects=True, vmem_limit_bytes=48 * 1024 * 1024
        ),
    )(
        *operands, edge_count
    )
    return pl.pallas_call(
        functools.partial(write_kernel, scale),
        out_shape=(
            jax.ShapeDtypeStruct((rows, feat), bf16),
            jax.ShapeDtypeStruct((hid, 2 * width), f32),
            jax.ShapeDtypeStruct((hid, width), f32),
        ),
        in_specs=[spec, spec],
        out_specs=(hbm, hbm, hbm),
        scratch_shapes=[vm((hid, 2 * width), f32), vm((hid, width), f32), dma((3,))],
        compiler_params=pltpu.CompilerParams(vmem_limit_bytes=4 * 1024 * 1024),
    )(node, total)


def layer(node_state, cotangent, w_in, w_out, send_list, sender, receiver, edge_count):
    parts = lax.axis_size("dom")
    fits = (
        node_state.shape[1] % 128 == 0
        and node_state.shape[0] % 16 == 0
        and send_list.shape[2] % 16 == 0
        and parts % 2 == 0
        and w_in.shape[0] % (16 * parts) == 0
        and sender.shape[0] % 128 == 0
    )
    plan = fused if fits else per_device
    return plan(node_state, cotangent, w_in, w_out, send_list, sender, receiver, edge_count)


def solution(mesh):
    return jax.shard_map(
        layer,
        mesh=mesh,
        in_specs=(
            P("dom", "tensor"),
            P("dom", "tensor"),
            P("tensor", None),
            P("tensor", None),
            P("dom", None, None),
            P("dom"),
            P("dom"),
            P("dom"),
        ),
        out_specs=(P("dom", "tensor"), P("tensor", None), P("tensor", None)),
        check_vma=False,
    )
```

```python
import functools

import jax
import jax.numpy as jnp
from jax import lax
from jax.experimental import pallas as pl
from jax.experimental.pallas import tpu as pltpu
from jax.sharding import PartitionSpec as P


def shifted(value, axis, steps):
    count = lax.axis_size(axis)
    pairs = [(source, (source + steps) % count) for source in range(count)]
    return lax.ppermute(value, axis, pairs)


def contract_rows(left, right):
    return lax.dot_general(
        left, right, (((0,), (0,)), ((), ())), preferred_element_type=jnp.float32
    )


def contract_cols(left, right):
    return lax.dot_general(
        left, right, (((1,), (1,)), ((), ())), preferred_element_type=jnp.float32
    )


def neighbour_offsets(count):
    return [1, count - 1, 2, count - 2, 3, count - 3, count // 2]


def per_device(node_state, cotangent, w_in, w_out, send_list, sender, receiver, edge_count):
    local_rows = node_state.shape[0]
    slots = send_list.shape[2]
    peers = send_list.shape[1]
    parts = lax.axis_size("dom")
    offsets = neighbour_offsets(parts)
    my_list = send_list[0]
    arrived = []
    for which, offset in enumerate(offsets):
        arrived.append(shifted(node_state[my_list[which]], "dom", offset))
    incoming = jnp.concatenate(arrived, 0)
    table_part = jnp.concatenate([node_state, incoming], 0)
    table, cot_full = (
        lax.all_gather(table_part, "tensor", axis=1, tiled=True),
        lax.all_gather(cotangent, "tensor", axis=1, tiled=True),
    )
    width = table.shape[1]
    rows = table.shape[0]
    w_send = w_in[:, :width]
    w_recv = w_in[:, width:]
    sent = table[sender]
    recv = table[receiver]
    pre = contract_cols(sent, w_send) + contract_cols(recv, w_recv)
    sig = jax.nn.sigmoid(pre)
    act = (pre * sig).astype(jnp.bfloat16)
    slope = sig * (1.0 + pre * (1.0 - sig))
    live = (jnp.arange(sender.shape[0], dtype=jnp.int32) < edge_count[0]).astype(jnp.bfloat16)
    message_grad = cot_full[receiver] * live[:, None]
    out_grad = contract_rows(act, message_grad)
    hidden_grad = contract_cols(message_grad, w_out)
    pre_grad = (hidden_grad * slope).astype(jnp.bfloat16)
    in_grad = jnp.concatenate([contract_rows(pre_grad, sent), contract_rows(pre_grad, recv)], 1)
    hit_send = (sender[:, None] == jnp.arange(rows, dtype=jnp.int32)[None, :]).astype(jnp.bfloat16)
    hit_recv = (receiver[:, None] == jnp.arange(local_rows, dtype=jnp.int32)[None, :]).astype(
        jnp.bfloat16
    )
    send_sum = contract_rows(hit_send, pre_grad).astype(jnp.bfloat16)
    recv_sum = contract_rows(hit_recv, pre_grad).astype(jnp.bfloat16)
    term = jnp.dot(send_sum, w_send, preferred_element_type=jnp.float32)
    term = term.at[:local_rows].add(jnp.dot(recv_sum, w_recv, preferred_element_type=jnp.float32))
    row_grad = lax.psum_scatter(term, "tensor", scatter_dimension=1, tiled=True)
    feat_part = row_grad.shape[1]
    halo_grad = row_grad[local_rows:].reshape(peers, slots, feat_part)
    node_grad = cotangent.astype(jnp.float32) + row_grad[:local_rows]
    for which, offset in enumerate(offsets):
        returned = shifted(halo_grad[which], "dom", parts - offset)
        node_grad = node_grad.at[my_list[which]].add(returned)
    sum_in, sum_out = lax.psum((in_grad, out_grad), "dom")
    scale = float(sender.shape[0] * parts) ** (-0.5)
    return (node_grad.astype(jnp.bfloat16), sum_in * scale, sum_out * scale)


MESH = pl.DeviceIdType.MESH


def dot(left, right):
    return jnp.dot(left, right, preferred_element_type=jnp.float32)


def split(value):
    high = value.astype(jnp.bfloat16)
    low = (value - high.astype(jnp.float32)).astype(jnp.bfloat16)
    return jnp.concatenate([high, low], 0)


def layer_kernel(
    parts, tps, offsets, slots,
    x_ref, c_ref, win_any, wout_any, list_any, send_any, recv_any, count_ref,
    node_ref, ag_ref,
    win_ref, wout_ref, list_ref, send_ref, recv_ref, spot_ref, load_s, xf, cf, st_loc, st_hal, rt, lt, ap, pre_buf, hid_buf,
    halo_out, halo_in, back_out, back_in, sums, rs, ag_out, ag, part_f, part_b, part_in,
    gx_s, gx_r, gc_s, gc_r, h_s, h_r, b_s, b_r, rs_s, rs_r, ag_s, ag_r, p_s, p_r, mid_out, mid_in, m_s, m_r,
):
    me = lax.axis_index("dom")
    mt = lax.axis_index("tensor")
    rows, feat = x_ref.shape
    hid = win_ref.shape[0]
    width = feat * tps
    edges = send_ref.shape[0]
    peers = len(offsets)
    halos = peers * slots
    squad = parts // 2
    seat = lax.rem(me, squad)
    base = me - seat
    chunk = hid // squad
    tile = 512 if edges % 512 == 0 else edges
    tiles = [slice(i, i + tile) for i in range(0, edges, tile)]

    def mod(value, count):
        return lax.rem(value + count, count)

    def copy(src, dst, ss, rsem, **where):
        return pltpu.make_async_remote_copy(
            src_ref=src, dst_ref=dst, send_sem=ss, recv_sem=rsem,
            device_id=where, device_id_type=MESH,
        )

    barrier = pltpu.get_barrier_semaphore()
    for k in range(1, tps):
        pl.semaphore_signal(barrier, inc=1, device_id={"tensor": mod(mt + k, tps)}, device_id_type=MESH)
    for k in range(1, parts):
        pl.semaphore_signal(barrier, inc=1, device_id={"dom": mod(me + k, parts)}, device_id_type=MESH)

    mine = pl.ds(pl.multiple_of(mt * feat, feat), feat)
    pairs = [
        (list_any, list_ref), (send_any, send_ref), (recv_any, recv_ref),
        (x_ref, xf.at[:, mine]), (win_any, win_ref), (c_ref, cf.at[:, mine]), (wout_any, wout_ref),
    ]
    loads = [pltpu.make_async_copy(a, b, load_s.at[i]) for i, (a, b) in enumerate(pairs)]
    for item in loads:
        item.start()
    pl.semaphore_wait(barrier, tps - 1 + parts - 1)

    x_copies = [
        copy(x_ref, xf.at[:, mine], gx_s.at[k], gx_r.at[k], tensor=mod(mt + k, tps))
        for k in range(1, tps)
    ]
    c_copies = [
        copy(c_ref, cf.at[:, mine], gc_s.at[k], gc_r.at[k], tensor=mod(mt + k, tps))
        for k in range(1, tps)
    ]
    for item in x_copies + c_copies:
        item.start()

    def hits(index, first, count):
        lanes = index.shape[1]
        spot = lax.broadcasted_iota(jnp.int32, (count, lanes), 0) + first
        return jnp.where(spot == index, 1.0, 0.0).astype(jnp.bfloat16)

    for item in loads[:3]:
        item.wait()
    for j in range(peers):
        spot_ref[:, j * slots:(j + 1) * slots] = list_ref[j]
    lt[...] = hits(spot_ref[...], 0, rows)
    count = count_ref[0]
    for cols in tiles:
        where = lax.broadcasted_iota(jnp.int32, (1, tile), 1) + cols.start
        target = jnp.where(where < count, recv_ref[cols].reshape(1, tile), -1)
        rt[:, cols] = hits(target, 0, rows)
        sends = send_ref[cols].reshape(1, tile)
        st_loc[:, cols] = hits(sends, 0, rows)
        st_hal[:, cols] = hits(sends, rows, halos)

    for item in loads[3:5]:
        item.wait()
    for item in x_copies:
        item.wait_recv()
    own = split(contract_cols(win_ref[:, :width], xf[...]))
    picked = dot(own, lt[...])
    halo_out[...] = (picked[:hid] + picked[hid:]).T
    h_copies = []
    for j, offset in enumerate(offsets):
        band = slice(j * slots, (j + 1) * slots)
        item = copy(
            halo_out.at[band], halo_in.at[band], h_s.at[j], h_r.at[j],
            dom=mod(me + offset, parts),
        )
        item.start()
        h_copies.append(item)

    at_recv = split(contract_cols(win_ref[:, width:], xf[...]))
    for cols in tiles:
        both = dot(own, st_loc[:, cols]) + dot(at_recv, rt[:, cols])
        pre_buf[:, cols] = both[:hid] + both[hid:]
    for item in loads[5:]:
        item.wait()
    for item in c_copies:
        item.wait_recv()
    grad = split(contract_cols(wout_ref[...], cf[...]))
    for cols in tiles:
        both = dot(grad, rt[:, cols])
        hid_buf[:, cols] = both[:hid] + both[hid:]

    for item in h_copies:
        item.wait_recv()
    far = split(halo_in[...].T)
    for cols in tiles:
        both = dot(far, st_hal[:, cols])
        pre = pre_buf[:, cols] + both[:hid] + both[hid:]
        sig = 0.5 * jnp.tanh(0.5 * pre) + 0.5
        slope = sig * (1.0 + pre * (1.0 - sig))
        ap[:hid, cols] = (pre * sig).astype(jnp.bfloat16)
        ap[hid:, cols] = (hid_buf[:, cols] * slope).astype(jnp.bfloat16)

    back_out[...] = contract_cols(st_hal[...], ap[hid:]).astype(jnp.bfloat16)
    b_copies = []
    for j, offset in enumerate(offsets):
        band = slice(j * slots, (j + 1) * slots)
        item = copy(
            back_out.at[band], back_in.at[band], b_s.at[j], b_r.at[j],
            dom=mod(me - offset, parts),
        )
        item.start()
        b_copies.append(item)

    spans = [slice(2 * width, 3 * width), slice(width, 2 * width), slice(0, width)]

    def scatter(which):
        out = []
        for k in range(1, squad):
            peer = mod(seat + k, squad)
            band = pl.ds(pl.multiple_of(peer * chunk, chunk), chunk)
            item = copy(
                sums.at[band, spans[which]], rs.at[k, :, spans[which]],
                rs_s.at[which, k], rs_r.at[which, k], dom=base + peer,
            )
            item.start()
            out.append(item)
        return out

    ours = pl.ds(pl.multiple_of(seat * chunk, chunk), chunk)

    def swap(which, arrivals):
        span = spans[which]
        total = sums[ours, span].astype(jnp.float32)
        for k, item in enumerate(arrivals):
            item.wait_recv()
            total = total + rs[k + 1, :, span].astype(jnp.float32)
        mid_out[:, span] = total.astype(jnp.bfloat16)
        item = copy(
            mid_out.at[:, span], mid_in.at[:, span], m_s.at[which], m_r.at[which],
            dom=mod(me + squad, parts),
        )
        item.start()
        return item

    def spread(which, arrival):
        span = spans[which]
        arrival.wait_recv()
        total = mid_out[:, span].astype(jnp.float32) + mid_in[:, span].astype(jnp.float32)
        total = total.astype(jnp.bfloat16)
        ag_out[:, span] = total
        ag[ours, span] = total
        out = []
        for k in range(1, squad):
            item = copy(
                ag_out.at[:, span], ag.at[ours, span],
                ag_s.at[which, k], ag_r.at[which, k], dom=base + mod(seat + k, squad),
            )
            item.start()
            out.append(item)
        return out

    at_node = contract_cols(ap[...], rt[...])
    act_sum = at_node[:hid].astype(jnp.bfloat16)
    recv_sum = at_node[hid:].astype(jnp.bfloat16)
    sums[:, 2 * width:] = dot(act_sum, cf[...]).astype(jnp.bfloat16)
    first = scatter(0)
    sums[:, width:2 * width] = dot(recv_sum, xf[...]).astype(jnp.bfloat16)
    second = scatter(1)
    near = contract_cols(ap[hid:], st_loc[...])
    part_f[...] = dot(at_node[hid:].T.astype(jnp.bfloat16), win_ref[:, width:])

    for item in b_copies:
        item.wait_recv()
    returned = back_in[...].astype(jnp.float32).T.astype(jnp.bfloat16)
    whole = near + contract_cols(returned, lt[...])
    sums[:, :width] = dot(whole.astype(jnp.bfloat16), xf[...]).astype(jnp.bfloat16)
    third = scatter(2)
    share = part_f[...] + dot(whole.T.astype(jnp.bfloat16), win_ref[:, :width])
    part_f[...] = share
    part_b[...] = share.astype(jnp.bfloat16)
    p_copies = []
    for k in range(1, tps):
        peer = mod(mt + k, tps)
        theirs = pl.ds(pl.multiple_of(peer * feat, feat), feat)
        item = copy(part_b.at[:, theirs], part_in.at[k], p_s.at[k], p_r.at[k], tensor=peer)
        item.start()
        p_copies.append(item)

    swaps = [swap(0, first), swap(1, second)]
    gathers = spread(0, swaps[0])
    swaps.append(swap(2, third))
    gathers += spread(1, swaps[1])
    node = cf[:, mine].astype(jnp.float32) + part_f[:, mine]
    for k, item in enumerate(p_copies):
        item.wait_recv()
        node = node + part_in[k + 1].astype(jnp.float32)
    node_ref[...] = node.astype(jnp.bfloat16)
    gathers += spread(2, swaps[2])
    for item in gathers:
        item.wait_recv()
    ag_ref[...] = ag[...]
    for item in x_copies + c_copies + h_copies + b_copies + first + second + third + p_copies + swaps + gathers:
        item.wait_send()


def write_kernel(scale, node_ref, ag_ref, node_any, gin_any, gout_any, gin_ref, gout_ref, sems):
    cut = gin_ref.shape[1]
    node_copy = pltpu.make_async_copy(node_ref, node_any, sems.at[0])
    node_copy.start()
    gin_ref[...] = ag_ref[:, :cut].astype(jnp.float32) * scale
    gin_copy = pltpu.make_async_copy(gin_ref, gin_any, sems.at[1])
    gin_copy.start()
    gout_ref[...] = ag_ref[:, cut:].astype(jnp.float32) * scale
    gout_copy = pltpu.make_async_copy(gout_ref, gout_any, sems.at[2])
    gout_copy.start()
    node_copy.wait()
    gin_copy.wait()
    gout_copy.wait()


def fused(node_state, cotangent, w_in, w_out, send_list, sender, receiver, edge_count):
    parts = lax.axis_size("dom")
    tps = lax.axis_size("tensor")
    rows, feat = node_state.shape
    hid = w_in.shape[0]
    width = feat * tps
    edges = sender.shape[0]
    _, peers, slots = send_list.shape
    halos = peers * slots
    offsets = neighbour_offsets(parts)
    squad = parts // 2
    chunk = hid // squad
    scale = float(edges * parts) ** (-0.5)
    bf16, f32 = jnp.bfloat16, jnp.float32
    vm, dma = pltpu.VMEM, pltpu.SemaphoreType.DMA
    spec = pl.BlockSpec(memory_space=pltpu.VMEM)
    hbm = pl.BlockSpec(memory_space=pltpu.HBM)
    operands = [
        pltpu.with_memory_space_constraint(item, pltpu.HBM)
        for item in (
            node_state, cotangent, w_in, w_out, send_list.transpose(1, 0, 2),
            sender, receiver,
        )
    ]
    node, total = pl.pallas_call(
        functools.partial(layer_kernel, parts, tps, offsets, slots),
        out_shape=(
            jax.ShapeDtypeStruct((rows, feat), bf16),
            jax.ShapeDtypeStruct((hid, 3 * width), bf16),
        ),
        in_specs=[hbm] * 7 + [pl.BlockSpec(memory_space=pltpu.SMEM)],
        out_specs=(spec, spec),
        scratch_shapes=[
            vm((hid, 2 * width), bf16),
            vm((hid, width), bf16),
            vm((peers, 1, slots), jnp.int32),
            vm((edges,), jnp.int32),
            vm((edges,), jnp.int32),
            vm((1, halos), jnp.int32),
            dma((7,)),
            vm((rows, width), bf16),
            vm((rows, width), bf16),
            vm((rows, edges), bf16),
            vm((halos, edges), bf16),
            vm((rows, edges), bf16),
            vm((rows, halos), bf16),
            vm((2 * hid, edges), bf16),
            vm((hid, edges), f32),
            vm((hid, edges), f32),
            vm((halos, hid), f32),
            vm((halos, hid), f32),
            vm((halos, hid), bf16),
            vm((halos, hid), bf16),
            vm((hid, 3 * width), bf16),
            vm((squad, chunk, 3 * width), bf16),
            vm((chunk, 3 * width), bf16),
            vm((hid, 3 * width), bf16),
            vm((rows, width), f32),
            vm((rows, width), bf16),
            vm((tps, rows, feat), bf16),
            dma((tps,)), dma((tps,)), dma((tps,)), dma((tps,)),
            dma((peers,)), dma((peers,)), dma((peers,)), dma((peers,)),
            dma((3, squad)), dma((3, squad)), dma((3, squad)), dma((3, squad)),
            dma((tps,)), dma((tps,)),
            vm((chunk, 3 * width), bf16), vm((chunk, 3 * width), bf16), dma((3,)), dma((3,)),
        ],
        compiler_params=pltpu.CompilerParams(
            collective_id=0, has_side_effects=True, vmem_limit_bytes=48 * 1024 * 1024
        ),
    )(
        *operands, edge_count
    )
    return pl.pallas_call(
        functools.partial(write_kernel, scale),
        out_shape=(
            jax.ShapeDtypeStruct((rows, feat), bf16),
            jax.ShapeDtypeStruct((hid, 2 * width), f32),
            jax.ShapeDtypeStruct((hid, width), f32),
        ),
        in_specs=[spec, spec],
        out_specs=(hbm, hbm, hbm),
        scratch_shapes=[vm((hid, 2 * width), f32), vm((hid, width), f32), dma((3,))],
        compiler_params=pltpu.CompilerParams(vmem_limit_bytes=4 * 1024 * 1024),
    )(node, total)


def layer(node_state, cotangent, w_in, w_out, send_list, sender, receiver, edge_count):
    parts = lax.axis_size("dom")
    fits = (
        node_state.shape[1] % 128 == 0
        and node_state.shape[0] % 16 == 0
        and send_list.shape[2] % 16 == 0
        and parts % 2 == 0
        and w_in.shape[0] % (16 * parts) == 0
        and sender.shape[0] % 128 == 0
    )
    plan = fused if fits else per_device
    return plan(node_state, cotangent, w_in, w_out, send_list, sender, receiver, edge_count)


def solution(mesh):
    return jax.shard_map(
        layer,
        mesh=mesh,
        in_specs=(
            P("dom", "tensor"),
            P("dom", "tensor"),
            P("tensor", None),
            P("tensor", None),
            P("dom", None, None),
            P("dom"),
            P("dom"),
            P("dom"),
        ),
        out_specs=(P("dom", "tensor"), P("tensor", None), P("tensor", None)),
        check_vma=False,
    )
```
